32 devices in a mesh: seq: 4 (over x, core), chan: 8 (over z, y).
Axes of the slice: x: 2, y: 2, z: 4, core: 2. Of those that a mesh axis runs over, the one named last changes fastest.
Arguments:
- inputs: bfloat16 [768, 262144], P('chan', 'seq'), may hold values from -6 to 6
- kernel: bfloat16 [768, 512, 512], P('chan', 'seq'), may hold values from -6 to 6
- forward_one: bfloat16 [512, 512], replicated, may hold values from -0.25 to 0.25
- forward_two: bfloat16 [512, 512], replicated, may hold values from -0.25 to 0.25
- inverse_one: bfloat16 [512, 512], replicated, may hold values from -0.25 to 0.25
- inverse_two: bfloat16 [512, 512], replicated, may hold values from -0.25 to 0.25
- norm_gain: float32 [768], replicated, may hold values from 0.1 to 1.9
- w_gate: bfloat16 [1536, 768], P('chan'), may hold values from -0.21875 to 0.21875
- w_up: bfloat16 [1536, 768], P('chan'), may hold values from -0.21875 to 0.21875
- w_down: bfloat16 [1536, 768], P('chan'), may hold values from -0.15625 to 0.15625
Outputs:
- output: bfloat16 [768, 262144], P('chan', 'seq')
The draws below stay inside these ranges and needn't reach their ends.
All inputs are finite; a program needn't handle non-finite values.
Results may differ from the reference program's by a relative error of at most 0.0075.
Values may be sent and summed in bfloat16 or wider, within the bound.
A program may use at most 192 MiB of HBM per device.

```python
import jax
import jax.numpy as jnp
from jax import lax

BLOCK = 512
CH = 768
FF = 1536
SEQ = 262144


def block_scale(stream_key, extent, cuts, least, top_value):
    loudness = 1.0
    for position, shards_of in cuts:
        heights = jax.random.uniform(jax.random.fold_in(jax.random.fold_in(stream_key, 6), position), (shards_of,), jnp.float32, least / len(cuts), top_value / len(cuts))
        loudness = loudness * jnp.repeat(jnp.exp(heights), extent[position] // shards_of).reshape((-1,) + (1,) * (len(extent) - 1 - position))
    return loudness


def gaussian(key, shape, width, most, split=(), dtype=jnp.bfloat16):
    drawn = jax.random.normal(key, shape, jnp.float32) * width
    if len(split) > 0:
        drawn = block_scale(key, shape, split, -0.22, 0.18) * drawn
    return jnp.clip(drawn, min=-most, max=most).astype(dtype)


def setup_inputs(seed: int = 0) -> dict:
    key_of = jax.random.split(jax.random.key(seed), 11)
    inputs = gaussian(key_of[0], (CH, SEQ), 1.0, 6.0, ((0, 8), (1, 4)))
    kernel = gaussian(key_of[1], (CH, BLOCK, BLOCK), 1.0, 6.0, ((0, 8), (1, 4)))
    forward_one = gaussian(key_of[2], (BLOCK, BLOCK), BLOCK ** -0.5, 0.25)
    forward_two = gaussian(key_of[3], (BLOCK, BLOCK), BLOCK ** -0.5, 0.25)
    inverse_one = gaussian(key_of[4], (BLOCK, BLOCK), BLOCK ** -0.5, 0.25)
    inverse_two = gaussian(key_of[5], (BLOCK, BLOCK), BLOCK ** -0.5, 0.25)
    norm_gain = jnp.clip(1.0 + 0.18 * jax.random.normal(key_of[6], (CH,), jnp.float32), 0.1, 1.9)
    w_gate = gaussian(key_of[7], (FF, CH), CH ** -0.5, 0.21875, ((0, 8),))
    w_up = gaussian(key_of[8], (FF, CH), CH ** -0.5, 0.21875, ((0, 8),))
    w_down = gaussian(key_of[9], (FF, CH), FF ** -0.5, 0.15625, ((0, 8),))
    return dict(inputs=inputs, kernel=kernel, forward_one=forward_one, forward_two=forward_two, inverse_one=inverse_one, inverse_two=inverse_two, norm_gain=norm_gain, w_gate=w_gate, w_up=w_up, w_down=w_down)


def mix_group(pieces, forward_one, forward_two, inverse_one, inverse_two):
    inputs_group, kernel_group = pieces
    count = inputs_group.shape[0]
    order = forward_one.shape[0]
    cube = inputs_group.reshape(count, order, order)
    first_section = jnp.einsum('cab,bk->cak', cube.astype(jnp.float32), forward_one.astype(jnp.float32)).astype(jnp.bfloat16)
    spectrum = jnp.einsum('cak,aj->ckj', first_section.astype(jnp.float32), forward_two.astype(jnp.float32))
    scaled = (spectrum * kernel_group.astype(jnp.float32)).astype(jnp.bfloat16)
    partial_inv = jnp.einsum('ckj,ji->cki', scaled.astype(jnp.float32), inverse_two.astype(jnp.float32)).astype(jnp.bfloat16)
    mixed_out = jnp.einsum('cki,km->cim', partial_inv.astype(jnp.float32), inverse_one.astype(jnp.float32))
    resid = (cube.astype(jnp.float32) + mixed_out).astype(jnp.bfloat16)
    return resid.reshape(count, order * order)

def mlp_block(stream_block, norm_gain, w_gate, w_up, w_down):
    stream = stream_block.astype(jnp.float32)
    mean_square = lax.optimization_barrier(jnp.mean(stream * stream, axis=0, keepdims=True))
    normed = (stream * lax.rsqrt(mean_square + 1e-05) * norm_gain[:, None]).astype(jnp.bfloat16)
    gate_part = jnp.dot(w_gate, normed, preferred_element_type=jnp.float32)
    up_part = jnp.dot(w_up, normed, preferred_element_type=jnp.float32)
    hidden = (jax.nn.gelu(gate_part, approximate=True) * up_part).astype(jnp.bfloat16)
    summed = jnp.dot(w_down.T, hidden, preferred_element_type=jnp.float32)
    return (stream + summed).astype(jnp.bfloat16)

def reference(inputs, kernel, forward_one, forward_two, inverse_one, inverse_two, norm_gain, w_gate, w_up, w_down):
    groups = 16
    per_group = CH // groups
    grouped_in = inputs.reshape(groups, per_group, SEQ)
    grouped_k = kernel.reshape(groups, per_group, BLOCK, BLOCK)
    resid = lax.map(lambda pieces: mix_group(pieces, forward_one, forward_two, inverse_one, inverse_two), (grouped_in, grouped_k))
    resid = resid.reshape(CH, BLOCK, BLOCK).transpose(1, 0, 2)
    outputs = lax.map(lambda blk: mlp_block(blk, norm_gain, w_gate, w_up, w_down), resid)
    return outputs.transpose(1, 0, 2).reshape(CH, SEQ)
```

```python
import functools

import jax
import jax.numpy as jnp
from jax import lax
from jax.experimental import pallas as pl
from jax.experimental.pallas import tpu as pltpu
from jax.sharding import PartitionSpec as P

MESH = pl.DeviceIdType.MESH
F32 = jnp.float32
BF16 = jnp.bfloat16
ROWS = 16


def greet(peers):
    barrier = pltpu.get_barrier_semaphore()
    for axis, count in peers:
        me = lax.axis_index(axis)
        for r in range(1, count):
            pl.semaphore_signal(
                barrier,
                inc=1,
                device_id={axis: lax.rem(me + r, count)},
                device_id_type=MESH,
            )
    pl.semaphore_wait(barrier, sum(count - 1 for _, count in peers))


def mix_kernel(
    nseq,
    nchan,
    x_hbm,
    kern_hbm,
    f1_ref,
    f2t_ref,
    i2t_ref,
    i1_ref,
    tok_hbm,
    xbuf,
    kbuf,
    send1,
    recv1,
    send2,
    recv2,
    zbuf,
    scr1,
    scr2,
    xsem,
    ksem,
    s1sem,
    r1sem,
    s2sem,
    r2sem,
    zssem,
    zrsem,
):
    order = f1_ref.shape[0]
    here = order // nseq
    per = here // nchan
    chans = x_hbm.shape[0]
    chunks = chans // ROWS
    me_s = lax.axis_index("seq")
    me_c = lax.axis_index("chan")

    def load_x(n):
        return pltpu.make_async_copy(
            x_hbm.at[pl.ds(n * ROWS, ROWS), :], xbuf.at[n % 4], xsem.at[n % 4]
        )

    def load_k(n):
        return pltpu.make_async_copy(
            kern_hbm.at[pl.ds(n * ROWS, ROWS)], kbuf.at[n % 2], ksem.at[n % 2]
        )

    def across(send, recv, ssem, rsem, n, r):
        to = lax.rem(me_s + r, nseq)
        return pltpu.make_async_remote_copy(
            src_ref=send.at[n % 2, to],
            dst_ref=recv.at[n % 3, me_s],
            send_sem=ssem.at[n % 2, r],
            recv_sem=rsem.at[n % 3, r],
            device_id={"seq": to},
            device_id_type=MESH,
        )

    def arrived(send, recv, ssem, rsem, n, r):
        source = lax.rem(me_s + nseq - r, nseq)
        return pltpu.make_async_remote_copy(
            src_ref=send.at[n % 2, source],
            dst_ref=recv.at[n % 3, source],
            send_sem=ssem.at[n % 2, r],
            recv_sem=rsem.at[n % 3, r],
            device_id={"seq": source},
            device_id_type=MESH,
        )

    def own(send, recv, ssem, n):
        return pltpu.make_async_copy(
            send.at[n % 2, me_s], recv.at[n % 3, me_s], ssem.at[n % 2, 0]
        )

    first = (send1, recv1, s1sem, r1sem)
    second = (send2, recv2, s2sem, r2sem)

    def start_all(stage, n):
        for r in range(1, nseq):
            across(*stage, n, r).start()
        own(stage[0], stage[1], stage[2], n).start()

    def wait_all(stage, n):
        own(stage[0], stage[1], stage[2], n).wait()
        for r in range(1, nseq):
            arrived(*stage, n, r).wait_recv()

    def wait_sent(stage, n):
        for r in range(1, nseq):
            across(*stage, n, r).wait_send()

    def z_copy(n, r):
        to = lax.rem(me_c + r, nchan)
        return pltpu.make_async_remote_copy(
            src_ref=zbuf.at[n % 2, to],
            dst_ref=tok_hbm.at[pl.ds(me_c * chans + n * ROWS, ROWS), :],
            send_sem=zssem.at[n % 2, r],
            recv_sem=zrsem.at[n, r],
            device_id={"chan": to},
            device_id_type=MESH,
        )

    def z_arrived(n, r):
        source = lax.rem(me_c + nchan - r, nchan)
        return pltpu.make_async_remote_copy(
            src_ref=zbuf.at[n % 2, source],
            dst_ref=tok_hbm.at[pl.ds(source * chans + n * ROWS, ROWS), :],
            send_sem=zssem.at[n % 2, r],
            recv_sem=zrsem.at[n, r],
            device_id={"chan": source},
            device_id_type=MESH,
        )

    def z_own(n):
        return pltpu.make_async_copy(
            zbuf.at[n % 2, me_c],
            tok_hbm.at[pl.ds(me_c * chans + n * ROWS, ROWS), :],
            zssem.at[n % 2, 0],
        )

    def stage_one(n):
        def body(g, carry):
            x = xbuf[n % 4, :, pl.ds(g * (ROWS * order), ROWS * order)]
            lhs = jnp.concatenate(
                [x[:, a * order : (a + 1) * order] for a in range(ROWS)], axis=0
            )
            out = jnp.dot(lhs, f1_ref[...], preferred_element_type=F32)
            for d in range(nseq):
                scr1[d * ROWS * ROWS : (d + 1) * ROWS * ROWS, :] = out[
                    :, d * here : (d + 1) * here
                ]
            for d in range(nseq):
                for c in range(ROWS):
                    v = scr1[pl.ds(d * ROWS * ROWS + c, ROWS, stride=ROWS), :]
                    send1[n % 2, d, c, pl.ds(g * ROWS, ROWS), :] = v.astype(BF16)
            return carry

        lax.fori_loop(0, here // ROWS, body, 0)

    def stage_two(n):
        def body(p, carry):
            c = 2 * p
            fs = jnp.concatenate(
                [
                    jnp.concatenate([recv1[n % 3, s, c + e] for s in range(nseq)], axis=0)
                    for e in range(2)
                ],
                axis=1,
            )
            spectrum = jnp.dot(f2t_ref[...], fs, preferred_element_type=F32)
            kern = jnp.concatenate([kbuf[n % 2, c], kbuf[n % 2, c + 1]], axis=0)
            scaled = (spectrum * kern.astype(F32).T).astype(BF16)
            inv = jnp.dot(i2t_ref[...], scaled, preferred_element_type=F32)
            for e in range(2):
                scr2[pl.ds(c + e, order, stride=ROWS), :] = inv[:, e * here : (e + 1) * here]
            return carry

        lax.fori_loop(0, ROWS // 2, body, 0)

        def cast(d, carry):
            send2[n % 2, d] = scr2[pl.ds(d * (here * ROWS), here * ROWS), :].astype(BF16)
            return carry

        lax.fori_loop(0, nseq, cast, 0)

    def stage_three(n):
        def body(step, carry):
            r = lax.rem(step + 1, nchan)
            to = lax.rem(me_c + r, nchan)

            @pl.when(jnp.logical_and(n >= 2, r > 0))
            def _():
                z_copy(n - 2, r).wait_send()

            @pl.when(jnp.logical_and(n >= 2, r == 0))
            def _():
                z_own(n - 2).wait()

            rows = pl.ds(to * (per * ROWS), per * ROWS)
            lhs = jnp.concatenate([recv2[n % 3, s, rows, :] for s in range(nseq)], axis=1)
            mixed = jnp.dot(lhs, i1_ref[...], preferred_element_type=F32)
            x = xbuf[n % 4, :, pl.ds(to * (per * order), per * order)].astype(F32)
            for i in range(per):
                cols = slice(i * order, (i + 1) * order)
                zbuf[n % 2, to, :, cols] = (
                    x[:, cols] + mixed[i * ROWS : (i + 1) * ROWS]
                ).astype(BF16)

            @pl.when(r > 0)
            def _():
                z_copy(n, r).start()

            @pl.when(r == 0)
            def _():
                z_own(n).start()

            return carry

        lax.fori_loop(0, nchan, body, 0)

    load_x(0).start()
    greet((("seq", nseq), ("chan", nchan)))

    def step(t, carry):
        @pl.when(t < chunks)
        def _():
            @pl.when(t + 1 < chunks)
            def _():
                load_x(t + 1).start()

            load_k(t).start()
            load_x(t).wait()

            @pl.when(t >= 2)
            def _():
                wait_sent(first, t - 2)

            stage_one(t)
            start_all(first, t)

        @pl.when(jnp.logical_and(t >= 1, t - 1 < chunks))
        def _():
            n = t - 1
            load_k(n).wait()
            wait_all(first, n)

            @pl.when(n >= 2)
            def _():
                wait_sent(second, n - 2)

            stage_two(n)
            start_all(second, n)

        @pl.when(t >= 2)
        def _():
            n = t - 2
            wait_all(second, n)
            stage_three(n)

        return carry

    lax.fori_loop(0, chunks + 2, step, 0)
    for n in range(max(chunks - 2, 0), chunks):
        wait_sent(first, n)
        wait_sent(second, n)
        z_own(n).wait()
        for r in range(1, nchan):
            z_copy(n, r).wait_send()

    def drain(n, carry):
        for r in range(1, nchan):
            z_arrived(n, r).wait_recv()
        return carry

    lax.fori_loop(0, chunks, drain, 0)


def mix(inputs, kernel, forward_one, forward_two, inverse_one, inverse_two, nseq, nchan):
    chans, here_positions = inputs.shape
    order = forward_one.shape[0]
    here = order // nseq
    chunks = chans // ROWS
    vmem = pl.BlockSpec(memory_space=pltpu.VMEM)
    hbm = pl.BlockSpec(memory_space=pl.ANY)
    elements = chans * here_positions
    return pl.pallas_call(
        functools.partial(mix_kernel, nseq, nchan),
        out_shape=jax.ShapeDtypeStruct((chans * nchan, here_positions // nchan), BF16),
        in_specs=[hbm, hbm, vmem, vmem, vmem, vmem],
        out_specs=hbm,
        scratch_shapes=[
            pltpu.VMEM((4, ROWS, here_positions), BF16),
            pltpu.VMEM((2, ROWS, here, order), BF16),
            pltpu.VMEM((2, nseq, ROWS, here, here), BF16),
            pltpu.VMEM((3, nseq, ROWS, here, here), BF16),
            pltpu.VMEM((2, nseq, here * ROWS, here), BF16),
            pltpu.VMEM((3, nseq, here * ROWS, here), BF16),
            pltpu.VMEM((2, nchan, ROWS, here_positions // nchan), BF16),
            pltpu.VMEM((nseq * ROWS * ROWS, here), F32),
            pltpu.VMEM((order * ROWS, here), F32),
            pltpu.SemaphoreType.DMA((4,)),
            pltpu.SemaphoreType.DMA((2,)),
            pltpu.SemaphoreType.DMA((2, nseq)),
            pltpu.SemaphoreType.DMA((3, nseq)),
            pltpu.SemaphoreType.DMA((2, nseq)),
            pltpu.SemaphoreType.DMA((3, nseq)),
            pltpu.SemaphoreType.DMA((2, nchan)),
            pltpu.SemaphoreType.DMA((chunks, nchan)),
        ],
        compiler_params=pltpu.CompilerParams(
            collective_id=0, has_side_effects=True, vmem_limit_bytes=56 * 2**20
        ),
        cost_estimate=pl.CostEstimate(
            flops=8 * elements * order, bytes_accessed=8 * elements, transcendentals=0
        ),
        name="mix",
    )(inputs, kernel, forward_one, forward_two.T, inverse_two.T, inverse_one)


SLOTS = 4
TILE = 512


def mlp_kernel(
    nchan,
    tok_ref,
    gain_ref,
    gate_ref,
    up_ref,
    down_ref,
    out_hbm,
    obuf,
    normed,
    total,
    ssem,
    rsem,
):
    t = pl.program_id(0)
    steps = pl.num_programs(0)
    me = lax.axis_index("chan")
    width = tok_ref.shape[0] // nchan
    held = out_hbm.shape[1] // nchan

    def send(n, r):
        to = lax.rem(me + r, nchan)
        return pltpu.make_async_remote_copy(
            src_ref=obuf.at[n % SLOTS, to],
            dst_ref=out_hbm.at[:, pl.ds(me * held + n * TILE, TILE)],
            send_sem=ssem.at[n % SLOTS, r],
            recv_sem=rsem.at[n, r],
            device_id={"chan": to},
            device_id_type=MESH,
        )

    def arrived(n, r):
        source = lax.rem(me + nchan - r, nchan)
        return pltpu.make_async_remote_copy(
            src_ref=obuf.at[n % SLOTS, source],
            dst_ref=out_hbm.at[:, pl.ds(source * held + n * TILE, TILE)],
            send_sem=ssem.at[n % SLOTS, r],
            recv_sem=rsem.at[n, r],
            device_id={"chan": source},
            device_id_type=MESH,
        )

    def own(n):
        return pltpu.make_async_copy(
            obuf.at[n % SLOTS, me],
            out_hbm.at[:, pl.ds(me * held + n * TILE, TILE)],
            ssem.at[n % SLOTS, 0],
        )

    def wait_sent(n):
        own(n).wait()
        for r in range(1, nchan):
            send(n, r).wait_send()

    @pl.when(t == 0)
    def _():
        greet((("chan", nchan),))

    x = tok_ref[...].astype(F32)
    mean_square = jnp.mean(x * x, axis=0, keepdims=True)
    normed[...] = (x * lax.rsqrt(mean_square + 1e-05) * gain_ref[...]).astype(BF16)
    total[...] = x

    def body(f, carry):
        gate = jnp.dot(gate_ref[f], normed[...], preferred_element_type=F32)
        up = jnp.dot(up_ref[f], normed[...], preferred_element_type=F32)
        act = 0.5 * gate * (1.0 + jnp.tanh(0.7978845608 * (gate + 0.044715 * gate * gate * gate)))
        hidden = (act * up).astype(BF16)
        total[...] += jnp.dot(down_ref[f], hidden, preferred_element_type=F32)
        return carry

    lax.fori_loop(0, gate_ref.shape[0], body, 0)

    @pl.when(t >= SLOTS)
    def _():
        wait_sent(t - SLOTS)

    for d in range(nchan):
        obuf[t % SLOTS, d] = total[d * width : (d + 1) * width, :].astype(BF16)
    for r in range(1, nchan):
        send(t, r).start()
    own(t).start()

    @pl.when(t == steps - 1)
    def _():
        def drain_sent(n, carry):
            wait_sent(n)
            return carry

        lax.fori_loop(steps - SLOTS, steps, drain_sent, 0)

        def drain(n, carry):
            for r in range(1, nchan):
                arrived(n, r).wait_recv()
            return carry

        lax.fori_loop(0, steps, drain, 0)


def mlp(tokens, norm_gain, gate_rows, up_rows, down_rows, nchan):
    width, held = tokens.shape
    hidden = gate_rows.shape[0]
    part = 256
    parts = hidden // part
    steps = held // TILE
    gate_rows = gate_rows.reshape(parts, part, width)
    up_rows = up_rows.reshape(parts, part, width)
    down_rows = down_rows.reshape(parts, part, width).transpose(0, 2, 1)
    whole = lambda *shape: pl.BlockSpec(shape, lambda t: (0,) * len(shape))
    return pl.pallas_call(
        functools.partial(mlp_kernel, nchan),
        out_shape=jax.ShapeDtypeStruct((width // nchan, held * nchan), BF16),
        grid=(steps,),
        in_specs=[
            pl.BlockSpec((width, TILE), lambda t: (0, t)),
            whole(width, 1),
            whole(parts, part, width),
            whole(parts, part, width),
            whole(parts, width, part),
        ],
        out_specs=pl.BlockSpec(memory_space=pl.ANY),
        scratch_shapes=[
            pltpu.VMEM((SLOTS, nchan, width // nchan, TILE), BF16),
            pltpu.VMEM((width, TILE), BF16),
            pltpu.VMEM((width, TILE), F32),
            pltpu.SemaphoreType.DMA((SLOTS, nchan)),
            pltpu.SemaphoreType.DMA((steps, nchan)),
        ],
        compiler_params=pltpu.CompilerParams(
            collective_id=1,
            has_side_effects=True,
            vmem_limit_bytes=48 * 2**20,
            dimension_semantics=("arbitrary",),
        ),
        cost_estimate=pl.CostEstimate(
            flops=6 * width * hidden * held,
            bytes_accessed=4 * width * held,
            transcendentals=hidden * held,
        ),
        name="mlp",
    )(tokens, norm_gain[:, None], gate_rows, up_rows, down_rows)


def shards(
    nseq,
    nchan,
    inputs,
    kernel,
    forward_one,
    forward_two,
    inverse_one,
    inverse_two,
    norm_gain,
    w_gate,
    w_up,
    w_down,
):
    gate_rows = lax.all_gather(w_gate, "chan", axis=0, tiled=True)
    up_rows = lax.all_gather(w_up, "chan", axis=0, tiled=True)
    down_rows = lax.all_gather(w_down, "chan", axis=0, tiled=True)
    tokens = mix(
        inputs, kernel, forward_one, forward_two, inverse_one, inverse_two, nseq, nchan
    )
    return mlp(tokens, norm_gain, gate_rows, up_rows, down_rows, nchan)


def plain_shards(
    inputs,
    kernel,
    forward_one,
    forward_two,
    inverse_one,
    inverse_two,
    norm_gain,
    w_gate,
    w_up,
    w_down,
):
    channels_here = inputs.shape[0]
    block_width = forward_one.shape[0]
    block_rows = inputs.shape[1] // block_width
    cube = inputs.reshape(channels_here, block_rows, block_width)
    first_section = jnp.einsum(
        "cab,bk->cak", cube, forward_one, preferred_element_type=jnp.float32
    ).astype(jnp.bfloat16)
    spectrum = jnp.einsum(
        "cak,aj->ckj",
        lax.all_to_all(first_section, "seq", split_axis=2, concat_axis=1, tiled=True),
        forward_two,
        preferred_element_type=jnp.float32,
    )
    scaled = (spectrum * kernel.astype(jnp.float32)).astype(jnp.bfloat16)
    partial_inv = jnp.einsum(
        "ckj,ji->cki", scaled, inverse_two, preferred_element_type=jnp.float32
    ).astype(jnp.bfloat16)
    mixed_out = jnp.einsum(
        "cki,km->cim",
        lax.all_to_all(partial_inv, "seq", split_axis=2, concat_axis=1, tiled=True),
        inverse_one,
        preferred_element_type=jnp.float32,
    )
    resid = (cube.astype(jnp.float32) + mixed_out).astype(jnp.bfloat16)
    resid = resid.reshape(channels_here, block_rows * block_width)
    tokens = lax.all_to_all(resid, "chan", split_axis=1, concat_axis=0, tiled=True)
    stream = tokens.astype(jnp.float32)
    mean_square = jnp.mean(stream * stream, axis=0, keepdims=True)
    normed = (stream * lax.rsqrt(mean_square + 1e-05) * norm_gain[:, None]).astype(jnp.bfloat16)
    gate_rows = lax.all_gather(w_gate, "chan", axis=0, tiled=True)
    up_rows = lax.all_gather(w_up, "chan", axis=0, tiled=True)
    down_rows = lax.all_gather(w_down, "chan", axis=0, tiled=True)
    gate_part = jnp.dot(gate_rows, normed, preferred_element_type=jnp.float32)
    up_part = jnp.dot(up_rows, normed, preferred_element_type=jnp.float32)
    hidden = (jax.nn.gelu(gate_part, approximate=True) * up_part).astype(jnp.bfloat16)
    summed = lax.dot_general(
        down_rows, hidden, (((0,), (0,)), ((), ())), preferred_element_type=jnp.float32
    )
    result = (stream + summed).astype(jnp.bfloat16)
    return lax.all_to_all(result, "chan", split_axis=0, concat_axis=1, tiled=True)


def solution(mesh):
    nseq, nchan = mesh.shape["seq"], mesh.shape["chan"]

    def body(inputs, kernel, forward_one, *rest):
        here = forward_one.shape[0] // nseq
        if here % 128 == 0 and here // nchan == ROWS and inputs.shape[0] % ROWS == 0:
            return shards(nseq, nchan, inputs, kernel, forward_one, *rest)
        return plain_shards(inputs, kernel, forward_one, *rest)

    return jax.shard_map(
        body,
        mesh=mesh,
        in_specs=(
            P("chan", "seq"),
            P("chan", "seq", None),
            P(),
            P(),
            P(),
            P(),
            P(),
            P("chan", None),
            P("chan", None),
            P("chan", None),
        ),
        out_specs=P("chan", "seq"),
        check_vma=False,
    )
```

```python
import functools

import jax
import jax.numpy as jnp
from jax import lax
from jax.experimental import pallas as pl
from jax.experimental.pallas import tpu as pltpu
from jax.sharding import PartitionSpec as P

MESH = pl.DeviceIdType.MESH
F32 = jnp.float32
BF16 = jnp.bfloat16
ROWS = 16
TILE = 512
SLOTS = 2


def greet(peers):
    barrier = pltpu.get_barrier_semaphore()
    for axis, count in peers:
        me = lax.axis_index(axis)
        for r in range(1, count):
            pl.semaphore_signal(
                barrier,
                inc=1,
                device_id={axis: lax.rem(me + r, count)},
                device_id_type=MESH,
            )
    pl.semaphore_wait(barrier, sum(count - 1 for _, count in peers))


def layer_kernel(
    nseq,
    nchan,
    x_hbm,
    kern_hbm,
    f1_ref,
    f2_ref,
    i2_ref,
    i1_ref,
    gain_ref,
    gate_hbm,
    up_hbm,
    down_hbm,
    tok_hbm,
    out_hbm,
    f2t_ref,
    i2t_ref,
    wbuf,
    downt,
    tbuf,
    obuf,
    normed,
    total,
    xbuf,
    kbuf,
    send1,
    recv1,
    send2,
    recv2,
    zbuf,
    scr1,
    scr2,
    xsem,
    ksem,
    s1sem,
    r1sem,
    s2sem,
    r2sem,
    zssem,
    zrsem,
    wlsem,
    w1ssem,
    w1rsem,
    w23sem,
    tsem,
    ossem,
    orsem,
):
    order = f1_ref.shape[0]
    here = order // nseq
    per = here // nchan
    chans = x_hbm.shape[0]
    chunks = chans // ROWS
    me_s = lax.axis_index("seq")
    me_c = lax.axis_index("chan")

    def load_x(n):
        return pltpu.make_async_copy(
            x_hbm.at[pl.ds(n * ROWS, ROWS), :], xbuf.at[n % 4], xsem.at[n % 4]
        )

    def load_k(n):
        return pltpu.make_async_copy(
            kern_hbm.at[pl.ds(n * ROWS, ROWS)], kbuf.at[n % 2], ksem.at[n % 2]
        )

    def across(send, recv, ssem, rsem, n, r):
        to = lax.rem(me_s + r, nseq)
        return pltpu.make_async_remote_copy(
            src_ref=send.at[n % 2, to],
            dst_ref=recv.at[n % 3, me_s],
            send_sem=ssem.at[n % 2, r],
            recv_sem=rsem.at[n % 3, r],
            device_id={"seq": to},
            device_id_type=MESH,
        )

    def arrived(send, recv, ssem, rsem, n, r):
        source = lax.rem(me_s + nseq - r, nseq)
        return pltpu.make_async_remote_copy(
            src_ref=send.at[n % 2, source],
            dst_ref=recv.at[n % 3, source],
            send_sem=ssem.at[n % 2, r],
            recv_sem=rsem.at[n % 3, r],
            device_id={"seq": source},
            device_id_type=MESH,
        )

    def own(send, recv, ssem, n):
        return pltpu.make_async_copy(
            send.at[n % 2, me_s], recv.at[n % 3, me_s], ssem.at[n % 2, 0]
        )

    first = (send1, recv1, s1sem, r1sem)
    second = (send2, recv2, s2sem, r2sem)

    def start_all(stage, n):
        for r in range(1, nseq):
            across(*stage, n, r).start()
        own(stage[0], stage[1], stage[2], n).start()

    def wait_all(stage, n):
        own(stage[0], stage[1], stage[2], n).wait()
        for r in range(1, nseq):
            arrived(*stage, n, r).wait_recv()

    def wait_sent(stage, n):
        for r in range(1, nseq):
            across(*stage, n, r).wait_send()

    def z_copy(n, r):
        to = lax.rem(me_c + r, nchan)
        return pltpu.make_async_remote_copy(
            src_ref=zbuf.at[n % 2, to],
            dst_ref=tok_hbm.at[pl.ds(me_c * chans + n * ROWS, ROWS), :],
            send_sem=zssem.at[n % 2, r],
            recv_sem=zrsem.at[n, r],
            device_id={"chan": to},
            device_id_type=MESH,
        )

    def z_arrived(n, r):
        source = lax.rem(me_c + nchan - r, nchan)
        return pltpu.make_async_remote_copy(
            src_ref=zbuf.at[n % 2, source],
            dst_ref=tok_hbm.at[pl.ds(source * chans + n * ROWS, ROWS), :],
            send_sem=zssem.at[n % 2, r],
            recv_sem=zrsem.at[n, r],
            device_id={"chan": source},
            device_id_type=MESH,
        )

    def z_own(n):
        return pltpu.make_async_copy(
            zbuf.at[n % 2, me_c],
            tok_hbm.at[pl.ds(me_c * chans + n * ROWS, ROWS), :],
            zssem.at[n % 2, 0],
        )

    pairs = nchan // 2
    zed, why = me_c // 2, me_c % 2
    half = me_s % 2
    mine = gate_hbm.shape[0] // 2
    weights = (gate_hbm, up_hbm, down_hbm)

    def w_own(j):
        return pltpu.make_async_copy(
            weights[j].at[pl.ds(half * mine, mine), :], wbuf.at[half, why, zed, j], wlsem.at[j]
        )

    def w_line(j, r):
        return pltpu.make_async_remote_copy(
            src_ref=weights[j].at[pl.ds(half * mine, mine), :],
            dst_ref=wbuf.at[half, why, zed, j],
            send_sem=w1ssem.at[j, r],
            recv_sem=w1rsem.at[j, r],
            device_id={"chan": lax.rem(zed + r, pairs) * 2 + why},
            device_id_type=MESH,
        )

    def w_line_arrived(j, r):
        source = lax.rem(zed + pairs - r, pairs)
        return pltpu.make_async_remote_copy(
            src_ref=weights[j].at[pl.ds(half * mine, mine), :],
            dst_ref=wbuf.at[half, why, source, j],
            send_sem=w1ssem.at[j, r],
            recv_sem=w1rsem.at[j, r],
            device_id={"chan": source * 2 + why},
            device_id_type=MESH,
        )

    def w_pair(side):
        return pltpu.make_async_remote_copy(
            src_ref=wbuf.at[half, side],
            dst_ref=wbuf.at[half, side],
            send_sem=w23sem.at[0],
            recv_sem=w23sem.at[1],
            device_id={"chan": me_c + 1 - 2 * why},
            device_id_type=MESH,
        )

    def w_cores(side):
        return pltpu.make_async_remote_copy(
            src_ref=wbuf.at[side],
            dst_ref=wbuf.at[side],
            send_sem=w23sem.at[2],
            recv_sem=w23sem.at[3],
            device_id={"seq": me_s + 1 - 2 * half},
            device_id_type=MESH,
        )

    held = out_hbm.shape[1] // nchan
    tiles = held // TILE

    def load_tile(t):
        return pltpu.make_async_copy(
            tok_hbm.at[:, pl.ds(t * TILE, TILE)], tbuf.at[t % 2], tsem.at[t % 2]
        )

    def o_copy(t, r):
        to = lax.rem(me_c + r, nchan)
        return pltpu.make_async_remote_copy(
            src_ref=obuf.at[t % SLOTS, to],
            dst_ref=out_hbm.at[:, pl.ds(me_c * held + t * TILE, TILE)],
            send_sem=ossem.at[t % SLOTS, r],
            recv_sem=orsem.at[t, r],
            device_id={"chan": to},
            device_id_type=MESH,
        )

    def o_arrived(t, r):
        source = lax.rem(me_c + nchan - r, nchan)
        return pltpu.make_async_remote_copy(
            src_ref=obuf.at[t % SLOTS, source],
            dst_ref=out_hbm.at[:, pl.ds(source * held + t * TILE, TILE)],
            send_sem=ossem.at[t % SLOTS, r],
            recv_sem=orsem.at[t, r],
            device_id={"chan": source},
            device_id_type=MESH,
        )

    def o_own(t):
        return pltpu.make_async_copy(
            obuf.at[t % SLOTS, me_c],
            out_hbm.at[:, pl.ds(me_c * held + t * TILE, TILE)],
            ossem.at[t % SLOTS, 0],
        )

    def o_sent(t):
        o_own(t).wait()
        for r in range(1, nchan):
            o_copy(t, r).wait_send()

    def mlp_tile(t, carry):
        @pl.when(t + 1 < tiles)
        def _():
            load_tile(t + 1).start()

        load_tile(t).wait()
        x = tbuf[t % 2].astype(F32)
        mean_square = jnp.mean(x * x, axis=0, keepdims=True)
        normed[...] = (x * lax.rsqrt(mean_square + 1e-05) * gain_ref[...]).astype(BF16)
        total[...] = x

        def body(f, carry):
            h, y = f // 2, f % 2
            gate_rows = jnp.concatenate([wbuf[h, y, z, 0] for z in range(pairs)], axis=0)
            up_rows = jnp.concatenate([wbuf[h, y, z, 1] for z in range(pairs)], axis=0)
            gate = jnp.dot(gate_rows, normed[...], preferred_element_type=F32)
            up = jnp.dot(up_rows, normed[...], preferred_element_type=F32)
            act = (
                0.5 * gate * (1.0 + jnp.tanh(0.7978845608 * (gate + 0.044715 * gate * gate * gate)))
            )
            hidden = (act * up).astype(BF16)
            total[...] += jnp.dot(downt[f], hidden, preferred_element_type=F32)
            return carry

        lax.fori_loop(0, 4, body, 0)

        @pl.when(t >= SLOTS)
        def _():
            o_sent(t - SLOTS)

        for d in range(nchan):
            obuf[t % SLOTS, d] = total[d * chans : (d + 1) * chans, :].astype(BF16)
        for r in range(1, nchan):
            o_copy(t, r).start()
        o_own(t).start()
        return carry

    def stage_one(n):
        def body(g, carry):
            x = xbuf[n % 4, :, pl.ds(g * (ROWS * order), ROWS * order)]
            lhs = jnp.concatenate(
                [x[:, a * order : (a + 1) * order] for a in range(ROWS)], axis=0
            )
            out = jnp.dot(lhs, f1_ref[...], preferred_element_type=F32)
            for d in range(nseq):
                scr1[d * ROWS * ROWS : (d + 1) * ROWS * ROWS, :] = out[
                    :, d * here : (d + 1) * here
                ]
            for d in range(nseq):
                for c in range(ROWS):
                    v = scr1[pl.ds(d * ROWS * ROWS + c, ROWS, stride=ROWS), :]
                    send1[n % 2, d, c, pl.ds(g * ROWS, ROWS), :] = v.astype(BF16)
            return carry

        lax.fori_loop(0, here // ROWS, body, 0)

    def stage_two(n):
        def body(p, carry):
            c = 2 * p
            fs = jnp.concatenate(
                [
                    jnp.concatenate([recv1[n % 3, s, c + e] for s in range(nseq)], axis=0)
                    for e in range(2)
                ],
                axis=1,
            )
            spectrum = jnp.dot(f2t_ref[...], fs, preferred_element_type=F32)
            kern = jnp.concatenate([kbuf[n % 2, c], kbuf[n % 2, c + 1]], axis=0)
            scaled = (spectrum * kern.astype(F32).T).astype(BF16)
            inv = jnp.dot(i2t_ref[...], scaled, preferred_element_type=F32)
            for e in range(2):
                scr2[pl.ds(c + e, order, stride=ROWS), :] = inv[:, e * here : (e + 1) * here]
            return carry

        lax.fori_loop(0, ROWS // 2, body, 0)

        def cast(d, carry):
            send2[n % 2, d] = scr2[pl.ds(d * (here * ROWS), here * ROWS), :].astype(BF16)
            return carry

        lax.fori_loop(0, nseq, cast, 0)

    def stage_three(n):
        def body(step, carry):
            r = lax.rem(step + 1, nchan)
            to = lax.rem(me_c + r, nchan)

            @pl.when(jnp.logical_and(n >= 2, r > 0))
            def _():
                z_copy(n - 2, r).wait_send()

            @pl.when(jnp.logical_and(n >= 2, r == 0))
            def _():
                z_own(n - 2).wait()

            rows = pl.ds(to * (per * ROWS), per * ROWS)
            lhs = jnp.concatenate([recv2[n % 3, s, rows, :] for s in range(nseq)], axis=1)
            mixed = jnp.dot(lhs, i1_ref[...], preferred_element_type=F32)
            x = xbuf[n % 4, :, pl.ds(to * (per * order), per * order)].astype(F32)
            for i in range(per):
                cols = slice(i * order, (i + 1) * order)
                zbuf[n % 2, to, :, cols] = (
                    x[:, cols] + mixed[i * ROWS : (i + 1) * ROWS]
                ).astype(BF16)

            @pl.when(r > 0)
            def _():
                z_copy(n, r).start()

            @pl.when(r == 0)
            def _():
                z_own(n).start()

            return carry

        lax.fori_loop(0, nchan, body, 0)

    load_x(0).start()
    f2t_ref[...] = f2_ref[...].astype(F32).T.astype(BF16)
    i2t_ref[...] = i2_ref[...].astype(F32).T.astype(BF16)
    greet((("seq", nseq), ("chan", nchan)))
    for j in range(3):
        for r in range(1, pairs):
            w_line(j, r).start()
        w_own(j).start()

    def step(t, carry):
        @pl.when(t == 2)
        def _():
            for j in range(3):
                w_own(j).wait()
                for r in range(1, pairs):
                    w_line_arrived(j, r).wait_recv()
            w_pair(why).start()

        @pl.when(t == 4)
        def _():
            w_pair(1 - why).wait_recv()
            w_cores(half).start()

        @pl.when(t < chunks)
        def _():
            @pl.when(t + 1 < chunks)
            def _():
                load_x(t + 1).start()

            load_k(t).start()
            load_x(t).wait()

            @pl.when(t >= 2)
            def _():
                wait_sent(first, t - 2)

            stage_one(t)
            start_all(first, t)

        @pl.when(jnp.logical_and(t >= 1, t - 1 < chunks))
        def _():
            n = t - 1
            load_k(n).wait()
            wait_all(first, n)

            @pl.when(n >= 2)
            def _():
                wait_sent(second, n - 2)

            stage_two(n)
            start_all(second, n)

        @pl.when(t >= 2)
        def _():
            n = t - 2
            wait_all(second, n)
            stage_three(n)

        return carry

    lax.fori_loop(0, chunks + 2, step, 0)
    for j in range(3):
        for r in range(1, pairs):
            w_line(j, r).wait_send()
    w_pair(why).wait_send()
    w_cores(half).wait_send()
    w_cores(1 - half).wait_recv()
    for f in range(4):
        rows = jnp.concatenate([wbuf[f // 2, f % 2, z, 2] for z in range(pairs)], axis=0)
        downt[f] = rows.astype(F32).T.astype(BF16)

    for n in range(max(chunks - 2, 0), chunks):
        wait_sent(first, n)
        wait_sent(second, n)
        z_own(n).wait()
        for r in range(1, nchan):
            z_copy(n, r).wait_send()

    def drain(n, carry):
        for r in range(1, nchan):
            z_arrived(n, r).wait_recv()
        return carry

    lax.fori_loop(0, chunks, drain, 0)
    load_tile(0).start()
    lax.fori_loop(0, tiles, mlp_tile, 0)
    for t in range(tiles - SLOTS, tiles):
        o_sent(t)

    def drain_out(t, carry):
        for r in range(1, nchan):
            o_arrived(t, r).wait_recv()
        return carry

    lax.fori_loop(0, tiles, drain_out, 0)


def shards(
    nseq,
    nchan,
    inputs,
    kernel,
    forward_one,
    forward_two,
    inverse_one,
    inverse_two,
    norm_gain,
    w_gate,
    w_up,
    w_down,
):
    chans, positions = inputs.shape
    order = forward_one.shape[0]
    here = order // nseq
    chunks = chans // ROWS
    held = positions // nchan
    width = chans * nchan
    rows = w_gate.shape[0]
    vmem = pl.BlockSpec(memory_space=pltpu.VMEM)
    hbm = pl.BlockSpec(memory_space=pl.ANY)
    elements = chans * positions
    _, result = pl.pallas_call(
        functools.partial(layer_kernel, nseq, nchan),
        out_shape=[
            jax.ShapeDtypeStruct((width, held), BF16),
            jax.ShapeDtypeStruct((chans, positions), BF16),
        ],
        in_specs=[hbm, hbm, vmem, vmem, vmem, vmem, vmem, hbm, hbm, hbm],
        out_specs=[hbm, hbm],
        scratch_shapes=[
            pltpu.VMEM((order, order), BF16),
            pltpu.VMEM((order, order), BF16),
            pltpu.VMEM((2, 2, nchan // 2, 3, rows // 2, width), BF16),
            pltpu.VMEM((4, width, rows * nchan // 4), BF16),
            pltpu.VMEM((2, width, TILE), BF16),
            pltpu.VMEM((SLOTS, nchan, chans, TILE), BF16),
            pltpu.VMEM((width, TILE), BF16),
            pltpu.VMEM((width, TILE), F32),
            pltpu.VMEM((4, ROWS, positions), BF16),
            pltpu.VMEM((2, ROWS, here, order), BF16),
            pltpu.VMEM((2, nseq, ROWS, here, here), BF16),
            pltpu.VMEM((3, nseq, ROWS, here, here), BF16),
            pltpu.VMEM((2, nseq, here * ROWS, here), BF16),
            pltpu.VMEM((3, nseq, here * ROWS, here), BF16),
            pltpu.VMEM((2, nchan, ROWS, held), BF16),
            pltpu.VMEM((nseq * ROWS * ROWS, here), F32),
            pltpu.VMEM((order * ROWS, here), F32),
            pltpu.SemaphoreType.DMA((4,)),
            pltpu.SemaphoreType.DMA((2,)),
            pltpu.SemaphoreType.DMA((2, nseq)),
            pltpu.SemaphoreType.DMA((3, nseq)),
            pltpu.SemaphoreType.DMA((2, nseq)),
            pltpu.SemaphoreType.DMA((3, nseq)),
            pltpu.SemaphoreType.DMA((2, nchan)),
            pltpu.SemaphoreType.DMA((chunks, nchan)),
            pltpu.SemaphoreType.DMA((3,)),
            pltpu.SemaphoreType.DMA((3, nchan // 2)),
            pltpu.SemaphoreType.DMA((3, nchan // 2)),
            pltpu.SemaphoreType.DMA((4,)),
            pltpu.SemaphoreType.DMA((2,)),
            pltpu.SemaphoreType.DMA((SLOTS, nchan)),
            pltpu.SemaphoreType.DMA((held // TILE, nchan)),
        ],
        compiler_params=pltpu.CompilerParams(
            collective_id=0, has_side_effects=True, vmem_limit_bytes=62 * 2**20
        ),
        cost_estimate=pl.CostEstimate(
            flops=8 * elements * order + 6 * rows * nchan * elements,
            bytes_accessed=12 * elements,
            transcendentals=rows * elements // chans,
        ),
        name="layer",
    )(
        inputs,
        kernel,
        forward_one,
        forward_two,
        inverse_two,
        inverse_one,
        norm_gain[:, None],
        w_gate,
        w_up,
        w_down,
    )
    return result


def plain_shards(
    inputs,
    kernel,
    forward_one,
    forward_two,
    inverse_one,
    inverse_two,
    norm_gain,
    w_gate,
    w_up,
    w_down,
):
    channels_here = inputs.shape[0]
    block_width = forward_one.shape[0]
    block_rows = inputs.shape[1] // block_width
    cube = inputs.reshape(channels_here, block_rows, block_width)
    first_section = jnp.einsum(
        "cab,bk->cak", cube, forward_one, preferred_element_type=jnp.float32
    ).astype(jnp.bfloat16)
    spectrum = jnp.einsum(
        "cak,aj->ckj",
        lax.all_to_all(first_section, "seq", split_axis=2, concat_axis=1, tiled=True),
        forward_two,
        preferred_element_type=jnp.float32,
    )
    scaled = (spectrum * kernel.astype(jnp.float32)).astype(jnp.bfloat16)
    partial_inv = jnp.einsum(
        "ckj,ji->cki", scaled, inverse_two, preferred_element_type=jnp.float32
    ).astype(jnp.bfloat16)
    mixed_out = jnp.einsum(
        "cki,km->cim",
        lax.all_to_all(partial_inv, "seq", split_axis=2, concat_axis=1, tiled=True),
        inverse_one,
        preferred_element_type=jnp.float32,
    )
    resid = (cube.astype(jnp.float32) + mixed_out).astype(jnp.bfloat16)
    resid = resid.reshape(channels_here, block_rows * block_width)
    tokens = lax.all_to_all(resid, "chan", split_axis=1, concat_axis=0, tiled=True)
    stream = tokens.astype(jnp.float32)
    mean_square = jnp.mean(stream * stream, axis=0, keepdims=True)
    normed = (stream * lax.rsqrt(mean_square + 1e-05) * norm_gain[:, None]).astype(jnp.bfloat16)
    gate_rows = lax.all_gather(w_gate, "chan", axis=0, tiled=True)
    up_rows = lax.all_gather(w_up, "chan", axis=0, tiled=True)
    down_rows = lax.all_gather(w_down, "chan", axis=0, tiled=True)
    gate_part = jnp.dot(gate_rows, normed, preferred_element_type=jnp.float32)
    up_part = jnp.dot(up_rows, normed, preferred_element_type=jnp.float32)
    hidden = (jax.nn.gelu(gate_part, approximate=True) * up_part).astype(jnp.bfloat16)
    summed = lax.dot_general(
        down_rows, hidden, (((0,), (0,)), ((), ())), preferred_element_type=jnp.float32
    )
    result = (stream + summed).astype(jnp.bfloat16)
    return lax.all_to_all(result, "chan", split_axis=0, concat_axis=1, tiled=True)


def solution(mesh):
    nseq, nchan = mesh.shape["seq"], mesh.shape["chan"]

    def body(inputs, kernel, forward_one, *rest):
        here = forward_one.shape[0] // nseq
        fits = here % 128 == 0 and here // nchan == ROWS and inputs.shape[0] % ROWS == 0
        fits = fits and nchan % 2 == 0 and rest[-1].shape[0] % 32 == 0
        if fits and inputs.shape[0] >= 6 * ROWS:
            return shards(nseq, nchan, inputs, kernel, forward_one, *rest)
        return plain_shards(inputs, kernel, forward_one, *rest)

    return jax.shard_map(
        body,
        mesh=mesh,
        in_specs=(
            P("chan", "seq"),
            P("chan", "seq", None),
            P(),
            P(),
            P(),
            P(),
            P(),
            P("chan", None),
            P("chan", None),
            P("chan", None),
        ),
        out_specs=P("chan", "seq"),
        check_vma=False,
    )
```

```python
import functools

import jax
import jax.numpy as jnp
from jax import lax
from jax.experimental import pallas as pl
from jax.experimental.pallas import tpu as pltpu
from jax.sharding import PartitionSpec as P

MESH = pl.DeviceIdType.MESH
F32 = jnp.float32
BF16 = jnp.bfloat16
ROWS = 16
TILE = 512
SLOTS = 2


def greet(peers):
    barrier = pltpu.get_barrier_semaphore()
    for axis, count in peers:
        me = lax.axis_index(axis)
        for r in range(1, count):
            pl.semaphore_signal(
                barrier,
                inc=1,
                device_id={axis: lax.rem(me + r, count)},
                device_id_type=MESH,
            )
    pl.semaphore_wait(barrier, sum(count - 1 for _, count in peers))


def layer_kernel(
    nseq,
    nchan,
    x_hbm,
    kern_hbm,
    f1_ref,
    f2_ref,
    i2_ref,
    i1_ref,
    gain_ref,
    gate_hbm,
    up_hbm,
    down_hbm,
    tok_hbm,
    out_hbm,
    f2t_ref,
    i2t_ref,
    wbuf,
    downt,
    tbuf,
    obuf,
    normed,
    total,
    xbuf,
    kbuf,
    send1,
    recv1,
    send2,
    recv2,
    zbuf,
    scr1,
    scr2,
    xsem,
    ksem,
    s1sem,
    r1sem,
    s2sem,
    r2sem,
    zssem,
    zrsem,
    wlsem,
    w1ssem,
    w1rsem,
    w23sem,
    tsem,
    ossem,
    orsem,
):
    order = f1_ref.shape[0]
    here = order // nseq
    per = here // nchan
    chans = x_hbm.shape[0]
    chunks = chans // ROWS
    me_s = lax.axis_index("seq")
    me_c = lax.axis_index("chan")

    def load_x(n):
        return pltpu.make_async_copy(
            x_hbm.at[pl.ds(n * ROWS, ROWS), :], xbuf.at[n % 4], xsem.at[n % 4]
        )

    def load_k(n):
        return pltpu.make_async_copy(
            kern_hbm.at[pl.ds(n * ROWS, ROWS)], kbuf.at[n % 2], ksem.at[n % 2]
        )

    def first_copy(n, r, part):
        to = lax.rem(me_s + r, nseq)
        some = pl.ds(part * (ROWS // 2), ROWS // 2)
        return pltpu.make_async_remote_copy(
            src_ref=send1.at[n % 2, to, some],
            dst_ref=recv1.at[n % 3, me_s, some],
            send_sem=s1sem.at[n % 2, r, part],
            recv_sem=r1sem.at[n % 3, r, part],
            device_id={"seq": to},
            device_id_type=MESH,
        )

    def first_arrived(n, r, part):
        source = lax.rem(me_s + nseq - r, nseq)
        some = pl.ds(part * (ROWS // 2), ROWS // 2)
        return pltpu.make_async_remote_copy(
            src_ref=send1.at[n % 2, source, some],
            dst_ref=recv1.at[n % 3, source, some],
            send_sem=s1sem.at[n % 2, r, part],
            recv_sem=r1sem.at[n % 3, r, part],
            device_id={"seq": source},
            device_id_type=MESH,
        )

    def first_own(n):
        return pltpu.make_async_copy(
            send1.at[n % 2, me_s], recv1.at[n % 3, me_s], s1sem.at[n % 2, 0, 0]
        )

    def start_first(n, part):
        for r in range(1, nseq):
            first_copy(n, r, part).start()

    def wait_first(n, part):
        for r in range(1, nseq):
            first_arrived(n, r, part).wait_recv()

    def first_sent(n):
        for part in range(2):
            for r in range(1, nseq):
                first_copy(n, r, part).wait_send()

    def piece(z):
        return pl.ds(lax.rem(me_c + z, nchan) * (per * ROWS), per * ROWS)

    def second_copy(n, r, z):
        to = lax.rem(me_s + r, nseq)
        return pltpu.make_async_remote_copy(
            src_ref=send2.at[n % 2, to, piece(z), :],
            dst_ref=recv2.at[n % 3, me_s, piece(z), :],
            send_sem=s2sem.at[n % 2, r, z],
            recv_sem=r2sem.at[n % 3, r, z],
            device_id={"seq": to},
            device_id_type=MESH,
        )

    def second_arrived(n, r, z):
        source = lax.rem(me_s + nseq - r, nseq)
        return pltpu.make_async_remote_copy(
            src_ref=send2.at[n % 2, source, piece(z), :],
            dst_ref=recv2.at[n % 3, source, piece(z), :],
            send_sem=s2sem.at[n % 2, r, z],
            recv_sem=r2sem.at[n % 3, r, z],
            device_id={"seq": source},
            device_id_type=MESH,
        )

    def second_own(n):
        return pltpu.make_async_copy(
            send2.at[n % 2, me_s], recv2.at[n % 3, me_s], s2sem.at[n % 2, 0, 0]
        )

    def start_second(n):
        second_own(n).start()

        def body(step, carry):
            for r in range(1, nseq):
                second_copy(n, r, lax.rem(step + 1, nchan)).start()
            return carry

        lax.fori_loop(0, nchan, body, 0)

    def second_sent(n):
        def body(z, carry):
            for r in range(1, nseq):
                second_copy(n, r, z).wait_send()
            return carry

        lax.fori_loop(0, nchan, body, 0)

    span = tok_hbm.shape[1] // 2

    def z_copy(n, r, part):
        to = lax.rem(me_c + r, nchan)
        some = pl.ds(part * span, span)
        return pltpu.make_async_remote_copy(
            src_ref=zbuf.at[n % 2, to, :, some],
            dst_ref=tok_hbm.at[pl.ds(me_c * chans + n * ROWS, ROWS), some],
            send_sem=zssem.at[n % 2, r, part],
            recv_sem=zrsem.at[n, r, part],
            device_id={"chan": to},
            device_id_type=MESH,
        )

    def z_arrived(n, r, part):
        source = lax.rem(me_c + nchan - r, nchan)
        some = pl.ds(part * span, span)
        return pltpu.make_async_remote_copy(
            src_ref=zbuf.at[n % 2, source, :, some],
            dst_ref=tok_hbm.at[pl.ds(source * chans + n * ROWS, ROWS), some],
            send_sem=zssem.at[n % 2, r, part],
            recv_sem=zrsem.at[n, r, part],
            device_id={"chan": source},
            device_id_type=MESH,
        )

    def z_own(n, part):
        some = pl.ds(part * span, span)
        return pltpu.make_async_copy(
            zbuf.at[n % 2, me_c, :, some],
            tok_hbm.at[pl.ds(me_c * chans + n * ROWS, ROWS), some],
            zssem.at[n % 2, 0, part],
        )

    pairs = nchan // 2
    zed, why = me_c // 2, me_c % 2
    half = me_s % 2
    mine = gate_hbm.shape[0] // 2
    weights = (gate_hbm, up_hbm, down_hbm)

    def w_own(j):
        return pltpu.make_async_copy(
            weights[j].at[pl.ds(half * mine, mine), :], wbuf.at[half, why, zed, j], wlsem.at[j]
        )

    def w_line(j, r):
        return pltpu.make_async_remote_copy(
            src_ref=weights[j].at[pl.ds(half * mine, mine), :],
            dst_ref=wbuf.at[half, why, zed, j],
            send_sem=w1ssem.at[j, r],
            recv_sem=w1rsem.at[j, r],
            device_id={"chan": lax.rem(zed + r, pairs) * 2 + why},
            device_id_type=MESH,
        )

    def w_line_arrived(j, r):
        source = lax.rem(zed + pairs - r, pairs)
        return pltpu.make_async_remote_copy(
            src_ref=weights[j].at[pl.ds(half * mine, mine), :],
            dst_ref=wbuf.at[half, why, source, j],
            send_sem=w1ssem.at[j, r],
            recv_sem=w1rsem.at[j, r],
            device_id={"chan": source * 2 + why},
            device_id_type=MESH,
        )

    def w_pair(side):
        return pltpu.make_async_remote_copy(
            src_ref=wbuf.at[half, side],
            dst_ref=wbuf.at[half, side],
            send_sem=w23sem.at[0],
            recv_sem=w23sem.at[1],
            device_id={"chan": me_c + 1 - 2 * why},
            device_id_type=MESH,
        )

    def w_cores(side):
        return pltpu.make_async_remote_copy(
            src_ref=wbuf.at[side],
            dst_ref=wbuf.at[side],
            send_sem=w23sem.at[2],
            recv_sem=w23sem.at[3],
            device_id={"seq": me_s + 1 - 2 * half},
            device_id_type=MESH,
        )

    held = out_hbm.shape[1] // nchan
    tiles = held // TILE

    def load_tile(t):
        return pltpu.make_async_copy(
            tok_hbm.at[:, pl.ds(t * TILE, TILE)], tbuf.at[t % 2], tsem.at[t % 2]
        )

    def o_copy(t, r):
        to = lax.rem(me_c + r, nchan)
        return pltpu.make_async_remote_copy(
            src_ref=obuf.at[t % SLOTS, to],
            dst_ref=out_hbm.at[:, pl.ds(me_c * held + t * TILE, TILE)],
            send_sem=ossem.at[t % SLOTS, r],
            recv_sem=orsem.at[t, r],
            device_id={"chan": to},
            device_id_type=MESH,
        )

    def o_arrived(t, r):
        source = lax.rem(me_c + nchan - r, nchan)
        return pltpu.make_async_remote_copy(
            src_ref=obuf.at[t % SLOTS, source],
            dst_ref=out_hbm.at[:, pl.ds(source * held + t * TILE, TILE)],
            send_sem=ossem.at[t % SLOTS, r],
            recv_sem=orsem.at[t, r],
            device_id={"chan": source},
            device_id_type=MESH,
        )

    def o_own(t):
        return pltpu.make_async_copy(
            obuf.at[t % SLOTS, me_c],
            out_hbm.at[:, pl.ds(me_c * held + t * TILE, TILE)],
            ossem.at[t % SLOTS, 0],
        )

    def o_sent(t):
        o_own(t).wait()
        for r in range(1, nchan):
            o_copy(t, r).wait_send()

    def mlp_tile(t, carry):
        @pl.when(lax.rem(t + 1, tiles // 2) > 0)
        def _():
            load_tile(t + 1).start()

        load_tile(t).wait()
        x = tbuf[t % 2].astype(F32)
        mean_square = jnp.mean(x * x, axis=0, keepdims=True)
        normed[...] = (x * lax.rsqrt(mean_square + 1e-05) * gain_ref[...]).astype(BF16)
        total[...] = x

        def body(f, carry):
            h, y = f // 2, f % 2
            gate_rows = jnp.concatenate([wbuf[h, y, z, 0] for z in range(pairs)], axis=0)
            up_rows = jnp.concatenate([wbuf[h, y, z, 1] for z in range(pairs)], axis=0)
            gate = jnp.dot(gate_rows, normed[...], preferred_element_type=F32)
            up = jnp.dot(up_rows, normed[...], preferred_element_type=F32)
            act = (
                0.5 * gate * (1.0 + jnp.tanh(0.7978845608 * (gate + 0.044715 * gate * gate * gate)))
            )
            hidden = (act * up).astype(BF16)
            total[...] += jnp.dot(downt[f], hidden, preferred_element_type=F32)
            return carry

        lax.fori_loop(0, 4, body, 0)

        @pl.when(t >= SLOTS)
        def _():
            o_sent(t - SLOTS)

        for d in range(nchan):
            obuf[t % SLOTS, d] = total[d * chans : (d + 1) * chans, :].astype(BF16)
        for r in range(1, nchan):
            o_copy(t, r).start()
        o_own(t).start()
        return carry

    def stage_one(n):
        def body(g, carry):
            x = xbuf[n % 4, :, pl.ds(g * (ROWS * order), ROWS * order)]
            lhs = jnp.concatenate(
                [x[:, a * order : (a + 1) * order] for a in range(ROWS)], axis=0
            )
            out = jnp.dot(lhs, f1_ref[...], preferred_element_type=F32)
            for d in range(nseq):
                scr1[d * ROWS * ROWS : (d + 1) * ROWS * ROWS, :] = out[
                    :, d * here : (d + 1) * here
                ]
            for d in range(nseq):
                for c in range(ROWS):
                    v = scr1[pl.ds(d * ROWS * ROWS + c, ROWS, stride=ROWS), :]
                    send1[n % 2, d, c, pl.ds(g * ROWS, ROWS), :] = v.astype(BF16)
            return carry

        lax.fori_loop(0, here // ROWS, body, 0)

    def stage_two(n):
        def body(p, carry):
            c = 2 * p
            fs = jnp.concatenate(
                [
                    jnp.concatenate([recv1[n % 3, s, c + e] for s in range(nseq)], axis=0)
                    for e in range(2)
                ],
                axis=1,
            )
            spectrum = jnp.dot(f2t_ref[...], fs, preferred_element_type=F32)
            kern = jnp.concatenate([kbuf[n % 2, c], kbuf[n % 2, c + 1]], axis=0)
            scaled = (spectrum * kern.astype(F32).T).astype(BF16)
            inv = jnp.dot(i2t_ref[...], scaled, preferred_element_type=F32)
            for e in range(2):
                scr2[pl.ds(c + e, order, stride=ROWS), :] = inv[:, e * here : (e + 1) * here]
            return carry

        wait_first(n, 0)
        lax.fori_loop(0, ROWS // 4, body, 0)
        wait_first(n, 1)
        lax.fori_loop(ROWS // 4, ROWS // 2, body, 0)

        def cast(d, carry):
            send2[n % 2, d] = scr2[pl.ds(d * (here * ROWS), here * ROWS), :].astype(BF16)
            return carry

        lax.fori_loop(0, nseq, cast, 0)

    def stage_three(n):
        some = per // 2

        def body(step, carry):
            part = step // nchan
            r = lax.rem(step + 1, nchan)
            to = lax.rem(me_c + r, nchan)

            @pl.when(part == 0)
            def _():
                for q in range(1, nseq):
                    second_arrived(n, q, r).wait_recv()

            @pl.when(jnp.logical_and(n >= 2, r > 0))
            def _():
                z_copy(n - 2, r, part).wait_send()

            rows = pl.ds((to * 2 + part) * (some * ROWS), some * ROWS)
            lhs = jnp.concatenate([recv2[n % 3, s, rows, :] for s in range(nseq)], axis=1)
            mixed = jnp.dot(lhs, i1_ref[...], preferred_element_type=F32)
            x = xbuf[n % 4, :, pl.ds((to * 2 + part) * span, span)].astype(F32)
            value = jnp.concatenate(
                [
                    x[:, i * order : (i + 1) * order] + mixed[i * ROWS : (i + 1) * ROWS]
                    for i in range(some)
                ],
                axis=1,
            )
            zbuf[n % 2, to, :, pl.ds(part * span, span)] = value.astype(BF16)

            @pl.when(r > 0)
            def _():
                z_copy(n, r, part).start()

            @pl.when(r == 0)
            def _():
                z_own(n, part).start()

            return carry

        @pl.when(n >= 2)
        def _():
            z_own(n - 2, 0).wait()
            z_own(n - 2, 1).wait()

        second_own(n).wait()
        lax.fori_loop(0, 2 * nchan, body, 0)

    load_x(0).start()
    f2t_ref[...] = f2_ref[...].astype(F32).T.astype(BF16)
    i2t_ref[...] = i2_ref[...].astype(F32).T.astype(BF16)
    greet((("seq", nseq), ("chan", nchan)))
    for j in range(3):
        for r in range(1, pairs):
            w_line(j, r).start()
        w_own(j).start()

    def step(t, carry):
        @pl.when(t == 2)
        def _():
            for j in range(3):
                w_own(j).wait()
                for r in range(1, pairs):
                    w_line_arrived(j, r).wait_recv()
            w_pair(why).start()

        @pl.when(t == 4)
        def _():
            w_pair(1 - why).wait_recv()
            w_cores(half).start()

        @pl.when(t < chunks)
        def _():
            @pl.when(t + 1 < chunks)
            def _():
                load_x(t + 1).start()

            load_k(t).start()
            load_x(t).wait()

            @pl.when(t >= 2)
            def _():
                first_sent(t - 2)

            stage_one(t)
            first_own(t).start()
            start_first(t, 0)

        @pl.when(t >= 2)
        def _():
            stage_three(t - 2)

        @pl.when(jnp.logical_and(t >= 1, t - 1 < chunks))
        def _():
            n = t - 1
            load_k(n).wait()
            first_own(n).wait()

            @pl.when(n >= 2)
            def _():
                second_sent(n - 2)

            stage_two(n)
            start_second(n)

        @pl.when(t < chunks)
        def _():
            start_first(t, 1)

        return carry

    lax.fori_loop(0, chunks + 2, step, 0)
    for j in range(3):
        for r in range(1, pairs):
            w_line(j, r).wait_send()
    w_pair(why).wait_send()
    w_cores(half).wait_send()
    w_cores(1 - half).wait_recv()
    for f in range(4):
        rows = jnp.concatenate([wbuf[f // 2, f % 2, z, 2] for z in range(pairs)], axis=0)
        downt[f] = rows.astype(F32).T.astype(BF16)

    def mlp_part(part, carry):
        def drain(n, carry):
            for r in range(1, nchan):
                z_arrived(n, r, part).wait_recv()
            return carry

        lax.fori_loop(0, chunks, drain, 0)

        @pl.when(part == 0)
        def _():
            for n in range(chunks - 2, chunks):
                z_own(n, 0).wait()
                z_own(n, 1).wait()

        load_tile(part * (tiles // 2)).start()
        lax.fori_loop(part * (tiles // 2), (part + 1) * (tiles // 2), mlp_tile, 0)
        return carry

    lax.fori_loop(0, 2, mlp_part, 0)
    for n in range(chunks - 2, chunks):
        first_sent(n)
        second_sent(n)
        for part in range(2):
            for r in range(1, nchan):
                z_copy(n, r, part).wait_send()

    for t in range(tiles - SLOTS, tiles):
        o_sent(t)

    def drain_out(t, carry):
        for r in range(1, nchan):
            o_arrived(t, r).wait_recv()
        return carry

    lax.fori_loop(0, tiles, drain_out, 0)


def shards(
    nseq,
    nchan,
    inputs,
    kernel,
    forward_one,
    forward_two,
    inverse_one,
    inverse_two,
    norm_gain,
    w_gate,
    w_up,
    w_down,
):
    chans, positions = inputs.shape
    order = forward_one.shape[0]
    here = order // nseq
    chunks = chans // ROWS
    held = positions // nchan
    width = chans * nchan
    rows = w_gate.shape[0]
    vmem = pl.BlockSpec(memory_space=pltpu.VMEM)
    hbm = pl.BlockSpec(memory_space=pl.ANY)
    elements = chans * positions
    _, result = pl.pallas_call(
        functools.partial(layer_kernel, nseq, nchan),
        out_shape=[
            jax.ShapeDtypeStruct((width, held), BF16),
            jax.ShapeDtypeStruct((chans, positions), BF16),
        ],
        in_specs=[hbm, hbm, vmem, vmem, vmem, vmem, vmem, hbm, hbm, hbm],
        out_specs=[hbm, hbm],
        scratch_shapes=[
            pltpu.VMEM((order, order), BF16),
            pltpu.VMEM((order, order), BF16),
            pltpu.VMEM((2, 2, nchan // 2, 3, rows // 2, width), BF16),
            pltpu.VMEM((4, width, rows * nchan // 4), BF16),
            pltpu.VMEM((2, width, TILE), BF16),
            pltpu.VMEM((SLOTS, nchan, chans, TILE), BF16),
            pltpu.VMEM((width, TILE), BF16),
            pltpu.VMEM((width, TILE), F32),
            pltpu.VMEM((4, ROWS, positions), BF16),
            pltpu.VMEM((2, ROWS, here, order), BF16),
            pltpu.VMEM((2, nseq, ROWS, here, here), BF16),
            pltpu.VMEM((3, nseq, ROWS, here, here), BF16),
            pltpu.VMEM((2, nseq, here * ROWS, here), BF16),
            pltpu.VMEM((3, nseq, here * ROWS, here), BF16),
            pltpu.VMEM((2, nchan, ROWS, held), BF16),
            pltpu.VMEM((nseq * ROWS * ROWS, here), F32),
            pltpu.VMEM((order * ROWS, here), F32),
            pltpu.SemaphoreType.DMA((4,)),
            pltpu.SemaphoreType.DMA((2,)),
            pltpu.SemaphoreType.DMA((2, nseq, 2)),
            pltpu.SemaphoreType.DMA((3, nseq, 2)),
            pltpu.SemaphoreType.DMA((2, nseq, nchan)),
            pltpu.SemaphoreType.DMA((3, nseq, nchan)),
            pltpu.SemaphoreType.DMA((2, nchan, 2)),
            pltpu.SemaphoreType.DMA((chunks, nchan, 2)),
            pltpu.SemaphoreType.DMA((3,)),
            pltpu.SemaphoreType.DMA((3, nchan // 2)),
            pltpu.SemaphoreType.DMA((3, nchan // 2)),
            pltpu.SemaphoreType.DMA((4,)),
            pltpu.SemaphoreType.DMA((2,)),
            pltpu.SemaphoreType.DMA((SLOTS, nchan)),
            pltpu.SemaphoreType.DMA((held // TILE, nchan)),
        ],
        compiler_params=pltpu.CompilerParams(
            collective_id=0, has_side_effects=True, vmem_limit_bytes=62 * 2**20
        ),
        cost_estimate=pl.CostEstimate(
            flops=8 * elements * order + 6 * rows * nchan * elements,
            bytes_accessed=12 * elements,
            transcendentals=rows * elements // chans,
        ),
        name="layer",
    )(
        inputs,
        kernel,
        forward_one,
        forward_two,
        inverse_two,
        inverse_one,
        norm_gain[:, None],
        w_gate,
        w_up,
        w_down,
    )
    return result


def plain_shards(
    inputs,
    kernel,
    forward_one,
    forward_two,
    inverse_one,
    inverse_two,
    norm_gain,
    w_gate,
    w_up,
    w_down,
):
    channels_here = inputs.shape[0]
    block_width = forward_one.shape[0]
    block_rows = inputs.shape[1] // block_width
    cube = inputs.reshape(channels_here, block_rows, block_width)
    first_section = jnp.einsum(
        "cab,bk->cak", cube, forward_one, preferred_element_type=jnp.float32
    ).astype(jnp.bfloat16)
    spectrum = jnp.einsum(
        "cak,aj->ckj",
        lax.all_to_all(first_section, "seq", split_axis=2, concat_axis=1, tiled=True),
        forward_two,
        preferred_element_type=jnp.float32,
    )
    scaled = (spectrum * kernel.astype(jnp.float32)).astype(jnp.bfloat16)
    partial_inv = jnp.einsum(
        "ckj,ji->cki", scaled, inverse_two, preferred_element_type=jnp.float32
    ).astype(jnp.bfloat16)
    mixed_out = jnp.einsum(
        "cki,km->cim",
        lax.all_to_all(partial_inv, "seq", split_axis=2, concat_axis=1, tiled=True),
        inverse_one,
        preferred_element_type=jnp.float32,
    )
    resid = (cube.astype(jnp.float32) + mixed_out).astype(jnp.bfloat16)
    resid = resid.reshape(channels_here, block_rows * block_width)
    tokens = lax.all_to_all(resid, "chan", split_axis=1, concat_axis=0, tiled=True)
    stream = tokens.astype(jnp.float32)
    mean_square = jnp.mean(stream * stream, axis=0, keepdims=True)
    normed = (stream * lax.rsqrt(mean_square + 1e-05) * norm_gain[:, None]).astype(jnp.bfloat16)
    gate_rows = lax.all_gather(w_gate, "chan", axis=0, tiled=True)
    up_rows = lax.all_gather(w_up, "chan", axis=0, tiled=True)
    down_rows = lax.all_gather(w_down, "chan", axis=0, tiled=True)
    gate_part = jnp.dot(gate_rows, normed, preferred_element_type=jnp.float32)
    up_part = jnp.dot(up_rows, normed, preferred_element_type=jnp.float32)
    hidden = (jax.nn.gelu(gate_part, approximate=True) * up_part).astype(jnp.bfloat16)
    summed = lax.dot_general(
        down_rows, hidden, (((0,), (0,)), ((), ())), preferred_element_type=jnp.float32
    )
    result = (stream + summed).astype(jnp.bfloat16)
    return lax.all_to_all(result, "chan", split_axis=0, concat_axis=1, tiled=True)


def solution(mesh):
    nseq, nchan = mesh.shape["seq"], mesh.shape["chan"]

    def body(inputs, kernel, forward_one, *rest):
        here = forward_one.shape[0] // nseq
        fits = here % 128 == 0 and here // nchan == ROWS and inputs.shape[0] % ROWS == 0
        fits = fits and nchan % 2 == 0 and rest[-1].shape[0] % 32 == 0
        if fits and inputs.shape[0] >= 6 * ROWS:
            return shards(nseq, nchan, inputs, kernel, forward_one, *rest)
        return plain_shards(inputs, kernel, forward_one, *rest)

    return jax.shard_map(
        body,
        mesh=mesh,
        in_specs=(
            P("chan", "seq"),
            P("chan", "seq", None),
            P(),
            P(),
            P(),
            P(),
            P(),
            P("chan", None),
            P("chan", None),
            P("chan", None),
        ),
        out_specs=P("chan", "seq"),
        check_vma=False,
    )
```
